256 devices in a mesh: row: 8 (over x, core), col: 32 (over y, z).
Axes of the slice: x: 4, y: 4, z: 8, core: 2. Of those that a mesh axis runs over, the one named last changes fastest.
Arguments:
- activations: bfloat16 [32768, 8192], P(('row', 'col')), may hold values from -24 to 24
- key_grads: bfloat16 [32768, 1024], P(('row', 'col')), may hold values from -24 to 24
- value_grads: bfloat16 [32768, 1024], P(('row', 'col')), may hold values from -24 to 24
- block_lengths: int32 [64], replicated, may hold values from 64 to 512, as said below
Outputs:
- key_clipped: bfloat16 [8192, 1024], P(('col', 'row'))
- value_clipped: bfloat16 [8192, 1024], P(('col', 'row'))
The draws below stay inside these ranges and needn't reach their ends.
Inputs may be any that keep to these rules, and one draw needn't show every extreme that they name: `block_lengths`: some block is full and some block holds 64 real tokens.
All inputs are finite; a program needn't handle non-finite values.
Results may differ from the reference program's by a relative error of at most 0.001.
Values may be sent and summed in bfloat16 or wider, within the bound.
No kernel may reach another device: no remote copies, remote signals or barrier semaphores. Data moves between devices by JAX's collectives and lax.ppermute only.
A program may use at most 64 MiB of HBM per device.

```python
import math
import jax
import jax.numpy as jnp
from jax import lax

D = 8192
F = 1024
CH = 512
LENGTH = 32768
NCHUNK = 64


def token_signs(base_key):
    sign_key = jax.random.fold_in(base_key, 97)
    drawn = jax.random.randint(sign_key, (LENGTH,), 0, 2, dtype=jnp.int32)
    return (2 * drawn - 1).astype(jnp.float32)


def scaled_field(key_scales, row_total, col_total, row_spread, base_field, signs, signed_weight):
    key_rows = jax.random.fold_in(key_scales, 0)
    key_cols = jax.random.fold_in(key_scales, 1)
    key_signed = jax.random.fold_in(key_scales, 3)
    rising = jnp.exp(math.log(3.0) * jnp.arange(row_total, dtype=jnp.float32) / row_total)
    row_factor = jnp.exp(jax.random.uniform(key_rows, (row_total,), jnp.float32, -row_spread, row_spread))
    col_factor = jnp.exp(jax.random.uniform(key_cols, (col_total,), jnp.float32, math.log(0.3), math.log(3.0)))
    shared_signed = jnp.clip(jax.random.normal(key_signed, (col_total,), jnp.float32), -3.0, 3.0)
    mixed = base_field + signed_weight * signs[:, None] * shared_signed[None, :]
    field = mixed * (rising * row_factor)[:, None] * col_factor[None, :]
    return jnp.clip(0.35 * field, -24.0, 24.0)


def draw_activations(key, part):
    signs = token_signs(key)
    key = jax.random.fold_in(key, 11)
    key_base, key_scales = jax.random.split(key)
    base_field = jnp.clip(jax.random.normal(key_base, (LENGTH, D), jnp.float32), -3.0, 3.0)
    field = scaled_field(key_scales, LENGTH, D, 0.7, base_field, signs, (0.5 / LENGTH) ** 0.25)
    return field.astype(jnp.bfloat16)


def draw_key_grads(key, part):
    signs = token_signs(key)
    key = jax.random.fold_in(key, 12)
    key_base, key_scales = jax.random.split(key)
    base_field = jnp.clip(jax.random.normal(key_base, (LENGTH, F), jnp.float32), -3.0, 3.0)
    field = scaled_field(key_scales, LENGTH, F, 0.7, base_field, signs, (0.5 / LENGTH) ** 0.25)
    return field.astype(jnp.bfloat16)


def draw_value_grads(key, part):
    signs = token_signs(key)
    key = jax.random.fold_in(key, 13)
    key_base, key_scales = jax.random.split(key)
    base_field = jnp.clip(jax.random.normal(key_base, (LENGTH, F), jnp.float32), -3.0, 3.0)
    field = scaled_field(key_scales, LENGTH, F, 0.7, base_field, signs, (0.5 / LENGTH) ** 0.25)
    return field.astype(jnp.bfloat16)


def draw_block_lengths(key, part):
    key = jax.random.fold_in(key, 14)
    key_values, key_full, key_short = jax.random.split(key, 3)
    drawn = jax.random.randint(key_values, (NCHUNK,), CH // 8, CH + 1, dtype=jnp.int32)
    full_at = jax.random.randint(key_full, (), 0, NCHUNK, dtype=jnp.int32)
    short_at = (full_at + jax.random.randint(key_short, (), 1, NCHUNK, dtype=jnp.int32)) % NCHUNK
    places = jnp.arange(NCHUNK, dtype=jnp.int32)
    drawn = jnp.where(places == full_at, CH, drawn)
    drawn = jnp.where(places == short_at, CH // 8, drawn)
    return drawn.astype(jnp.int32)


def setup_inputs(seed: int = 0) -> dict:
    keys = jax.random.split(jax.random.key(seed), 5)
    activations = draw_activations(jax.random.fold_in(keys[4], 71), 0)
    key_grads = draw_key_grads(jax.random.fold_in(keys[4], 71), 0)
    value_grads = draw_value_grads(jax.random.fold_in(keys[4], 71), 0)
    block_lengths = draw_block_lengths(jax.random.fold_in(keys[4], 71), 0)
    return {"activations": activations, "key_grads": key_grads, "value_grads": value_grads, "block_lengths": block_lengths}


def reference(activations, key_grads, value_grads, block_lengths):
    position = jnp.arange(activations.shape[0], dtype=jnp.int32)
    limit_len = block_lengths[position // CH]
    is_real = position % CH < limit_len
    keys_kept = jnp.where(is_real[:, None], key_grads, jnp.zeros_like(key_grads))
    values_kept = jnp.where(is_real[:, None], value_grads, jnp.zeros_like(value_grads))
    contract = (((0,), (0,)), ((), ()))
    key_weight = lax.dot_general(activations, keys_kept, contract, preferred_element_type=jnp.float32)
    value_weight = lax.dot_general(activations, values_kept, contract, preferred_element_type=jnp.float32)
    total = jnp.sum(key_weight * key_weight) + jnp.sum(value_weight * value_weight)
    clip_norm = math.sqrt(2.0 * activations.shape[1] * key_grads.shape[1])
    factor = jnp.minimum(1.0, clip_norm / jnp.sqrt(total))
    return ((factor * key_weight).astype(jnp.bfloat16), (factor * value_weight).astype(jnp.bfloat16))
```

```python
import itertools
import math

import jax
import jax.numpy as jnp
from jax import lax
from jax.sharding import Mesh, PartitionSpec as P

CH = 512
AXES = ("x", "c", "y", "z")
NX, NC, NY, NZ = 4, 2, 4, 8
CONTRACT = (((0,), (0,)), ((), ()))


def pairs(move):
    out = []
    for x, c, y, z in itertools.product(range(NX), range(NC), range(NY), range(NZ)):
        tx, tc, ty, tz = move(x, c, y, z)
        source = ((x * NC + c) * NY + y) * NZ + z
        target = (((tx % NX) * NC + tc % NC) * NY + ty % NY) * NZ + tz % NZ
        out.append((source, target))
    return out


def send(value, move):
    return lax.ppermute(value, AXES, pairs(move))


def swap_cores(value):
    return send(value, lambda x, c, y, z: (x, 1 - c, y, z))


def first_ring(value, step):
    return send(value, lambda x, c, y, z: (x + step, c, y, z) if c == 0 else (x, c, y + step, z))


def second_ring(value, step):
    return send(value, lambda x, c, y, z: (x, c, y + step, z) if c == 0 else (x + step, c, y, z))


def z_ring(value, step):
    return send(value, lambda x, c, y, z: (x, c, y, z + step))


def gather_ring(value, ring):
    half = value.shape[0] // 2
    before = ring(value, 1)
    after = ring(value, -1)
    opposite = jnp.concatenate((ring(before[:half], 1), ring(after[half:], -1)), axis=0)
    return value, before, after, opposite


OFFSETS = (0, -1, 1, 2)


def reduce_z(partial, z):
    rows = partial.shape[0] // NZ
    half = rows // 2

    def block(offset):
        return lax.dynamic_slice_in_dim(partial, lax.rem(z + offset + NZ, NZ) * rows, rows, axis=0)

    far = block(4)
    up = z_ring(far[:half], 1)
    down = z_ring(far[half:], -1)
    near_up, near_down = block(3), block(-3)
    up = z_ring(jnp.concatenate((near_up[:half] + up, near_up[half:]), axis=0), 1)
    down = z_ring(jnp.concatenate((near_down[:half], near_down[half:] + down), axis=0), -1)
    for offset in (2, 1):
        up = z_ring(block(offset) + up, 1)
        down = z_ring(block(-offset) + down, -1)
    return block(0) + up + down


def sum_all(value):
    value = value + swap_cores(value)
    for bit in (1, 2):
        value = value + send(value, lambda x, c, y, z: (x ^ bit, c, y, z))
    for bit in (1, 2):
        value = value + send(value, lambda x, c, y, z: (x, c, y ^ bit, z))
    for bit in (1, 2, 4):
        value = value + send(value, lambda x, c, y, z: (x, c, y, z ^ bit))
    return value


def body(activations, key_grads, value_grads, block_lengths):
    tok_count, model_width = activations.shape
    head_width = key_grads.shape[1]
    x, c, y, z = (lax.axis_index(axis) for axis in AXES)
    is_keys = c == 0
    position = (((x * NC + c) * NY + y) * NZ + z) * tok_count
    limit_len = lax.dynamic_index_in_dim(block_lengths, position // CH, keepdims=False)
    rows = lax.broadcasted_iota(jnp.int32, (tok_count, 1), 0)
    is_real = rows + lax.rem(position, CH) < limit_len
    clip_norm = math.sqrt(2.0 * model_width * head_width)

    zero = jnp.zeros((), key_grads.dtype)
    mine = jnp.where(is_real, jnp.where(is_keys, key_grads, value_grads), zero)
    theirs = jnp.where(is_real, jnp.where(is_keys, value_grads, key_grads), zero)
    grads = jnp.concatenate((mine, swap_cores(theirs)), axis=0)

    lump = jnp.concatenate(gather_ring(grads, first_ring), axis=0)

    acts = lax.all_to_all(activations, ("y", "x"), split_axis=1, concat_axis=0, tiled=True)
    acts_other = swap_cores(acts)
    acts = acts.reshape(NX * NY, tok_count, -1)
    acts_other = acts_other.reshape(NX * NY, tok_count, -1)

    first, second = jnp.where(is_keys, x, y), jnp.where(is_keys, y, x)
    weight = None
    for offset2, part in zip(OFFSETS, gather_ring(lump, second_ring)):
        blocks = []
        for offset1 in OFFSETS:
            at1, at2 = lax.rem(first + offset1 + 4, 4), lax.rem(second + offset2 + 4, 4)
            index = jnp.where(is_keys, at2 * NX + at1, at1 * NX + at2)
            blocks.append(lax.dynamic_index_in_dim(acts, index, keepdims=False))
            blocks.append(lax.dynamic_index_in_dim(acts_other, index, keepdims=False))
        product = lax.dot_general(
            jnp.concatenate(blocks, axis=0), part, CONTRACT, preferred_element_type=jnp.float32
        )
        weight = product if weight is None else weight + product

    owned = reduce_z(weight, z)
    squares = jnp.broadcast_to(jnp.sum(owned * owned), (8, 128))
    total = sum_all(squares)[0, 0]

    half = owned.shape[0] // 2
    low, high = owned[:half], owned[half:]
    same = send(
        jnp.where(is_keys, low, high), lambda x, c, y, z: (z % NX, c, y, 2 * x + z // NX)
    )
    cross = send(
        jnp.where(is_keys, high, low), lambda x, c, y, z: (z % NX, 1 - c, y, 2 * x + z // NX)
    )
    factor = jnp.minimum(1.0, clip_norm / jnp.sqrt(total))
    key_clipped = (jnp.where(is_keys, same, cross) * factor).astype(jnp.bfloat16)
    value_clipped = (jnp.where(is_keys, cross, same) * factor).astype(jnp.bfloat16)
    return key_clipped, value_clipped


def solution(mesh):
    fine = Mesh(mesh.devices.reshape(NX, NC, NY, NZ), AXES)
    tokens = P(AXES, None)
    owners = P(("y", "z", "x", "c"), None)
    return jax.shard_map(
        body,
        mesh=fine,
        in_specs=(tokens, tokens, tokens, P()),
        out_specs=(owners, owners),
        check_vma=False,
    )
```

```python
import itertools
import math

import jax
import jax.numpy as jnp
from jax import lax
from jax.experimental import pallas as pl
from jax.experimental.pallas import tpu as pltpu
from jax.sharding import Mesh, PartitionSpec as P

CH = 512
AXES = ("x", "c", "y", "z")
NX, NC, NY, NZ = 4, 2, 4, 8
DEVICES = NX * NC * NY * NZ
OFFSETS = (0, -1, 1, 2)
SPLITS = (512, 512)


def pairs(move):
    out = []
    for x, c, y, z in itertools.product(range(NX), range(NC), range(NY), range(NZ)):
        tx, tc, ty, tz = move(x, c, y, z)
        source = ((x * NC + c) * NY + y) * NZ + z
        target = (((tx % NX) * NC + tc % NC) * NY + ty % NY) * NZ + tz % NZ
        out.append((source, target))
    return out


def send(value, move):
    return lax.ppermute(value, AXES, pairs(move))


def swap_cores(value):
    return send(value, lambda x, c, y, z: (x, 1 - c, y, z))


def first_ring(value, step):
    return send(value, lambda x, c, y, z: (x + step, c, y, z) if c == 0 else (x, c, y + step, z))


def second_ring(value, step):
    return send(value, lambda x, c, y, z: (x, c, y + step, z) if c == 0 else (x + step, c, y, z))


def z_ring(value, step):
    return send(value, lambda x, c, y, z: (x, c, y, z + step))


def dot_kernel(offsets, has_start, index_ref, acts_ref, other_ref, *refs):
    out_ref = refs[-1]
    start_ref = refs[0] if has_start else None
    parts = refs[1:-1] if has_start else refs[:-1]
    total = start_ref[...] if has_start else None
    at = 0
    for part_ref in parts:
        for piece in range(part_ref.shape[0]):
            block = index_ref[offsets[at]]
            lhs = jnp.concatenate((acts_ref[block], other_ref[block]), axis=1)
            product = jnp.dot(lhs, part_ref[piece], preferred_element_type=jnp.float32)
            total = product if total is None else total + product
            at += 1
    out_ref[...] = total


def multiply(index, acts, other, parts, offsets, start=None):
    width, n = acts.shape[1], parts[0].shape[2]
    operands = [acts, other] + ([] if start is None else [start]) + list(parts)
    depth = sum(part.shape[0] * part.shape[1] for part in parts)
    vmem = pl.BlockSpec(memory_space=pltpu.VMEM)
    return pl.pallas_call(
        lambda *refs: dot_kernel(offsets, start is not None, *refs),
        out_shape=jax.ShapeDtypeStruct((width, n), jnp.float32),
        in_specs=[pl.BlockSpec(memory_space=pltpu.SMEM)] + [vmem] * len(operands),
        out_specs=vmem,
        compiler_params=pltpu.CompilerParams(vmem_limit_bytes=40 * 1024 * 1024),
        cost_estimate=pl.CostEstimate(
            flops=2 * width * n * depth, bytes_accessed=2 * depth * (n + width), transcendentals=0
        ),
    )(index, *operands)


def reduce_z(partial, z):
    rows = partial.shape[0] // NZ
    half = rows // 2

    def block(offset):
        return lax.dynamic_slice_in_dim(partial, lax.rem(z + offset + NZ, NZ) * rows, rows, axis=0)

    far = block(4)
    up = z_ring(far[:half], 1)
    down = z_ring(far[half:], -1)
    near_up, near_down = block(3), block(-3)
    up = z_ring(jnp.concatenate((near_up[:half] + up, near_up[half:]), axis=0), 1)
    down = z_ring(jnp.concatenate((near_down[:half], near_down[half:] + down), axis=0), -1)
    for offset in (2, 1):
        up = z_ring(block(offset) + up, 1)
        down = z_ring(block(-offset) + down, -1)
    return block(0) + up + down


def sum_all(value):
    rows = jnp.broadcast_to(value, (DEVICES, 1, 128))
    return jnp.sum(lax.all_to_all(rows, AXES, split_axis=0, concat_axis=0, tiled=True)[:, 0, 0])


def body(activations, key_grads, value_grads, block_lengths):
    tok_count, model_width = activations.shape
    head_width = key_grads.shape[1]
    x, c, y, z = (lax.axis_index(axis) for axis in AXES)
    is_keys = c == 0
    position = (((x * NC + c) * NY + y) * NZ + z) * tok_count
    limit_len = lax.dynamic_index_in_dim(block_lengths, position // CH, keepdims=False)
    rows = lax.broadcasted_iota(jnp.int32, (tok_count, 1), 0)
    is_real = rows + lax.rem(position, CH) < limit_len
    clip_norm = math.sqrt(2.0 * model_width * head_width)

    zero = jnp.zeros((), key_grads.dtype)
    mine = jnp.where(is_real, jnp.where(is_keys, key_grads, value_grads), zero)
    theirs = jnp.where(is_real, jnp.where(is_keys, value_grads, key_grads), zero)
    received = swap_cores(theirs)

    grads = jnp.stack((mine, received))
    before = first_ring(grads, 1)
    after = first_ring(grads, -1)
    opposite = (first_ring(before[:1], 1), first_ring(after[1:], -1))

    owner_rows = model_width // (NX * NY * NZ)
    across = activations.T.reshape(NY, NZ, NX, owner_rows, tok_count)
    across = across.transpose(0, 2, 1, 3, 4).reshape(NY * NX, NZ * owner_rows, tok_count)
    acts = lax.all_to_all(across, ("y", "x"), split_axis=0, concat_axis=0, tiled=True)
    other = swap_cores(acts)

    first, second = jnp.where(is_keys, x, y), jnp.where(is_keys, y, x)
    index = []
    for offset2 in OFFSETS:
        for offset1 in OFFSETS:
            at1, at2 = lax.rem(first + offset1 + 4, 4), lax.rem(second + offset2 + 4, 4)
            index.append(jnp.where(is_keys, at2 * NX + at1, at1 * NX + at2))
    index = jnp.stack(index).astype(jnp.int32)

    owned = []
    low = 0
    for columns in SPLITS:
        cut = slice(low, low + columns)
        low += columns
        lump = jnp.stack(
            (
                grads[:, :, cut],
                before[:, :, cut],
                after[:, :, cut],
                jnp.concatenate((opposite[0][:, :, cut], opposite[1][:, :, cut])),
            )
        ).reshape(4, 2 * tok_count, columns)
        lump_before = second_ring(lump, 1)
        lump_after = second_ring(lump, -1)
        opposite_a = second_ring(lump_before[:2], 1)
        opposite_b = second_ring(lump_after[2:], -1)
        weight = multiply(index, acts, other, [lump, lump_before, lump_after], range(12))
        weight = multiply(index, acts, other, [opposite_a, opposite_b], range(12, 16), weight)
        owned.append(reduce_z(weight, z))

    total = sum_all(sum(jnp.sum(part * part) for part in owned))
    owned = jnp.concatenate(owned, axis=1)
    half = owned.shape[0] // 2
    upper, lower = owned[:half], owned[half:]
    kept = jnp.where(is_keys, upper, lower)
    swapped = swap_cores(jnp.where(is_keys, lower, upper))
    factor = jnp.minimum(1.0, clip_norm / jnp.sqrt(total))
    key_clipped = (jnp.where(is_keys, kept, swapped) * factor).astype(jnp.bfloat16)
    value_clipped = (jnp.where(is_keys, swapped, kept) * factor).astype(jnp.bfloat16)
    return key_clipped, value_clipped


def solution(mesh):
    fine = Mesh(mesh.devices.reshape(NX, NC, NY, NZ), AXES)
    tokens = P(AXES, None)
    owners = P(("y", "z", "x", "c"), None)
    return jax.shard_map(
        body,
        mesh=fine,
        in_specs=(tokens, tokens, tokens, P()),
        out_specs=(owners, owners),
        check_vma=False,
    )
```

```python
import functools
import itertools
import math

import jax
import jax.numpy as jnp
from jax import lax
from jax.experimental import pallas as pl
from jax.experimental.pallas import tpu as pltpu
from jax.sharding import Mesh, PartitionSpec as P

CH = 512
AXES = ("x", "c", "y", "z")
NX, NC, NY, NZ = 4, 2, 4, 8
DEVICES = NX * NC * NY * NZ
OFFSETS = (0, -1, 1, 2)
SPLITS = (512, 512)


def pairs(move):
    out = []
    for x, c, y, z in itertools.product(range(NX), range(NC), range(NY), range(NZ)):
        tx, tc, ty, tz = move(x, c, y, z)
        source = ((x * NC + c) * NY + y) * NZ + z
        target = (((tx % NX) * NC + tc % NC) * NY + ty % NY) * NZ + tz % NZ
        out.append((source, target))
    return out


def send(value, move):
    return lax.ppermute(value, AXES, pairs(move))


def swap_cores(value):
    return send(value, lambda x, c, y, z: (x, 1 - c, y, z))


def first_ring(value, step):
    return send(value, lambda x, c, y, z: (x + step, c, y, z) if c == 0 else (x, c, y + step, z))


def second_ring(value, step):
    return send(value, lambda x, c, y, z: (x, c, y + step, z) if c == 0 else (x + step, c, y, z))


def z_ring(value, step):
    return send(value, lambda x, c, y, z: (x, c, y, z + step))


def mask_kernel(splits, place_ref, lengths_ref, keys_ref, values_ref, *out_refs):
    is_keys = place_ref[0] == 0
    limit = lengths_ref[place_ref[1]] - place_ref[2]
    low = 0
    for i, columns in enumerate(splits):
        cut = pl.ds(low, columns)
        low += columns
        keys, values = keys_ref[:, cut], values_ref[:, cut]
        rows = lax.broadcasted_iota(jnp.int32, keys.shape, 0)
        zero = jnp.zeros_like(keys)
        keys = jnp.where(rows < limit, keys, zero)
        values = jnp.where(rows < limit, values, zero)
        out_refs[2 * i][...] = jnp.where(is_keys, keys, values)
        out_refs[2 * i + 1][...] = jnp.where(is_keys, values, keys)


def mask(place, block_lengths, key_grads, value_grads):
    tok_count = key_grads.shape[0]
    smem = pl.BlockSpec(memory_space=pltpu.SMEM)
    vmem = pl.BlockSpec(memory_space=pltpu.VMEM)
    return pl.pallas_call(
        functools.partial(mask_kernel, SPLITS),
        out_shape=[
            jax.ShapeDtypeStruct((tok_count, columns), key_grads.dtype)
            for columns in SPLITS
            for _ in range(2)
        ],
        in_specs=[smem, smem, vmem, vmem],
        out_specs=[vmem] * (2 * len(SPLITS)),
        cost_estimate=pl.CostEstimate(
            flops=key_grads.size, bytes_accessed=8 * key_grads.size, transcendentals=0
        ),
    )(place, block_lengths, key_grads, value_grads)


def transpose_kernel(acts_ref, after_ref, out_ref):
    owner_rows = out_ref.shape[1] // NZ
    for at in range(0, acts_ref.shape[1], 128):
        turned = acts_ref[:, at : at + 128].T
        for low in range(0, 128, owner_rows):
            piece = (at + low) // owner_rows
            y, z, x = piece // (NZ * NX), piece // NX % NZ, piece % NX
            out_ref[y * NX + x, z * owner_rows : (z + 1) * owner_rows, :] = turned[
                low : low + owner_rows
            ]


def transpose(acts, after):
    tok_count, model_width = acts.shape
    vmem = pl.BlockSpec(memory_space=pltpu.VMEM)
    return pl.pallas_call(
        transpose_kernel,
        out_shape=jax.ShapeDtypeStruct(
            (NX * NY, model_width // (NX * NY), tok_count), acts.dtype
        ),
        in_specs=[vmem, pl.BlockSpec(memory_space=pl.ANY)],
        out_specs=vmem,
        compiler_params=pltpu.CompilerParams(vmem_limit_bytes=24 * 1024 * 1024),
        cost_estimate=pl.CostEstimate(
            flops=acts.size, bytes_accessed=4 * acts.size, transcendentals=0
        ),
    )(acts, after)


def dot_kernel(offsets, has_start, index_ref, acts_ref, other_ref, *refs):
    out_ref = refs[-1]
    start_ref = refs[0] if has_start else None
    parts = refs[1:-1] if has_start else refs[:-1]
    tile = 128
    for row in range(0, out_ref.shape[0], tile):
        cut = pl.ds(row, tile)
        total = start_ref[cut, :] if has_start else None
        for part_ref, places in zip(parts, offsets):
            blocks = []
            for place in places:
                block = index_ref[place]
                blocks += [acts_ref[block, cut, :], other_ref[block, cut, :]]
            product = jnp.dot(
                jnp.concatenate(blocks, axis=1), part_ref[...], preferred_element_type=jnp.float32
            )
            total = product if total is None else total + product
        out_ref[cut, :] = total


def multiply(index, acts, other, parts, offsets, start=None, after=()):
    width, n = acts.shape[1], parts[0].shape[1]
    operands = [acts, other] + ([] if start is None else [start]) + list(parts)
    depth = sum(part.shape[0] for part in parts)
    vmem = pl.BlockSpec(memory_space=pltpu.VMEM)

    def kernel(*refs):
        read = refs[: 1 + len(operands)]
        dot_kernel(offsets, start is not None, *read, refs[-1])

    return pl.pallas_call(
        kernel,
        out_shape=jax.ShapeDtypeStruct((width, n), jnp.float32),
        in_specs=[pl.BlockSpec(memory_space=pltpu.SMEM)]
        + [vmem] * len(operands)
        + [pl.BlockSpec(memory_space=pl.ANY)] * len(after),
        out_specs=vmem,
        compiler_params=pltpu.CompilerParams(vmem_limit_bytes=40 * 1024 * 1024),
        cost_estimate=pl.CostEstimate(
            flops=2 * width * n * depth, bytes_accessed=2 * depth * (n + width), transcendentals=0
        ),
    )(index, *operands, *after)


def reduce_z(partial, z):
    rows = partial.shape[0] // NZ
    half = rows // 2

    def block(offset):
        return lax.dynamic_slice_in_dim(partial, lax.rem(z + offset + NZ, NZ) * rows, rows, axis=0)

    far = block(4)
    up = z_ring(far[:half], 1)
    down = z_ring(far[half:], -1)
    near_up, near_down = block(3), block(-3)
    up = z_ring(jnp.concatenate((near_up[:half] + up, near_up[half:]), axis=0), 1)
    down = z_ring(jnp.concatenate((near_down[:half], near_down[half:] + down), axis=0), -1)
    for offset in (2, 1):
        up = z_ring(block(offset) + up, 1)
        down = z_ring(block(-offset) + down, -1)
    return block(0) + up + down


def sum_all(value):
    rows = jnp.broadcast_to(value, (DEVICES, 1, 128))
    return jnp.sum(lax.all_to_all(rows, AXES, split_axis=0, concat_axis=0, tiled=True)[:, 0, 0])


def body(activations, key_grads, value_grads, block_lengths):
    tok_count, model_width = activations.shape
    head_width = key_grads.shape[1]
    x, c, y, z = (lax.axis_index(axis) for axis in AXES)
    is_keys = c == 0
    position = (((x * NC + c) * NY + y) * NZ + z) * tok_count
    clip_norm = math.sqrt(2.0 * model_width * head_width)

    place = jnp.stack((c, lax.div(position, CH), lax.rem(position, CH))).astype(jnp.int32)
    masked = mask(place, block_lengths, key_grads, value_grads)
    grads, rings = [], []
    for mine, theirs in zip(masked[0::2], masked[1::2]):
        grads.append(jnp.concatenate((mine, swap_cores(theirs)), axis=0))
        rings.append((first_ring(grads[-1], 1), first_ring(grads[-1], -1)))

    across = transpose(activations, grads[-1])
    acts = lax.all_to_all(across, ("y", "x"), split_axis=0, concat_axis=0, tiled=True)
    other = swap_cores(acts)

    first, second = jnp.where(is_keys, x, y), jnp.where(is_keys, y, x)
    index = []
    for offset2 in OFFSETS:
        for offset1 in OFFSETS:
            at1, at2 = lax.rem(first + offset1 + 4, 4), lax.rem(second + offset2 + 4, 4)
            index.append(jnp.where(is_keys, at2 * NX + at1, at1 * NX + at2))
    index = jnp.stack(index).astype(jnp.int32)
    own, minus, plus, across_ring = (tuple(range(4 * i, 4 * i + 4)) for i in range(4))

    owned = []
    for part, (grad, (before, after)) in enumerate(zip(grads, rings)):
        step = 1 if part % 2 == 0 else -1
        opposite = first_ring(before if step == 1 else after, step)
        lump = jnp.concatenate((grad, before, after, opposite), axis=0)
        lump_before = second_ring(lump, 1)
        lump_after = second_ring(lump, -1)
        lump_opposite = second_ring(lump_before if step == 1 else lump_after, step)
        weight = multiply(
            index, acts, other, [lump, lump_before, lump_after], [own, minus, plus]
        )
        weight = multiply(index, acts, other, [lump_opposite], [across_ring], weight)
        owned.append(reduce_z(weight, z))

    total = sum_all(sum(jnp.sum(part * part) for part in owned))
    owned = jnp.concatenate(owned, axis=1)
    half = owned.shape[0] // 2
    upper, lower = owned[:half], owned[half:]
    kept = jnp.where(is_keys, upper, lower)
    swapped = swap_cores(jnp.where(is_keys, lower, upper))
    factor = jnp.minimum(1.0, clip_norm / jnp.sqrt(total))
    key_clipped = (jnp.where(is_keys, kept, swapped) * factor).astype(jnp.bfloat16)
    value_clipped = (jnp.where(is_keys, swapped, kept) * factor).astype(jnp.bfloat16)
    return key_clipped, value_clipped


def solution(mesh):
    fine = Mesh(mesh.devices.reshape(NX, NC, NY, NZ), AXES)
    tokens = P(AXES, None)
    owners = P(("y", "z", "x", "c"), None)
    return jax.shard_map(
        body,
        mesh=fine,
        in_specs=(tokens, tokens, tokens, P()),
        out_specs=(owners, owners),
        check_vma=False,
    )
```

```python
import functools
import itertools
import math

import jax
import jax.numpy as jnp
from jax import lax
from jax.experimental import pallas as pl
from jax.experimental.pallas import tpu as pltpu
from jax.sharding import Mesh, PartitionSpec as P

CH = 512
AXES = ("x", "c", "y", "z")
NX, NC, NY, NZ = 4, 2, 4, 8
DEVICES = NX * NC * NY * NZ
OFFSETS = (0, -1, 1, 2)
SPLITS = (512, 512)


def pairs(move):
    out = []
    for x, c, y, z in itertools.product(range(NX), range(NC), range(NY), range(NZ)):
        tx, tc, ty, tz = move(x, c, y, z)
        source = ((x * NC + c) * NY + y) * NZ + z
        target = (((tx % NX) * NC + tc % NC) * NY + ty % NY) * NZ + tz % NZ
        out.append((source, target))
    return out


def send(value, move):
    return lax.ppermute(value, AXES, pairs(move))


def swap_cores(value):
    return send(value, lambda x, c, y, z: (x, 1 - c, y, z))


def first_ring(value, step):
    return send(value, lambda x, c, y, z: (x + step, c, y, z) if c == 0 else (x, c, y + step, z))


def second_ring(value, step):
    return send(value, lambda x, c, y, z: (x, c, y + step, z) if c == 0 else (x + step, c, y, z))


def mask_kernel(place_ref, lengths_ref, keys_ref, values_ref, mine_ref, theirs_ref):
    is_keys = place_ref[0] == 0
    limit = lengths_ref[place_ref[1]] - place_ref[2]
    keys, values = keys_ref[...], values_ref[...]
    rows = lax.broadcasted_iota(jnp.int32, keys.shape, 0)
    zero = jnp.zeros_like(keys)
    keys = jnp.where(rows < limit, keys, zero)
    values = jnp.where(rows < limit, values, zero)
    mine_ref[...] = jnp.where(is_keys, keys, values)
    theirs_ref[...] = jnp.where(is_keys, values, keys)


def mask(place, block_lengths, key_grads, value_grads):
    smem = pl.BlockSpec(memory_space=pltpu.SMEM)
    vmem = pl.BlockSpec(memory_space=pltpu.VMEM)
    return pl.pallas_call(
        mask_kernel,
        out_shape=[jax.ShapeDtypeStruct(key_grads.shape, key_grads.dtype)] * 2,
        in_specs=[smem, smem, vmem, vmem],
        out_specs=[vmem, vmem],
        cost_estimate=pl.CostEstimate(
            flops=key_grads.size, bytes_accessed=8 * key_grads.size, transcendentals=0
        ),
    )(place, block_lengths, key_grads, value_grads)


def lump_kernel(*refs):
    outs = refs[-len(SPLITS) :]
    pieces = refs[: -len(SPLITS)]
    tok_count = pieces[0].shape[0]
    low = 0
    for columns, out_ref in zip(SPLITS, outs):
        for i, piece_ref in enumerate(pieces):
            out_ref[pl.ds(i * tok_count, tok_count), :] = piece_ref[:, pl.ds(low, columns)]
        low += columns


def lumps(pieces):
    rows = len(pieces) * pieces[0].shape[0]
    vmem = pl.BlockSpec(memory_space=pltpu.VMEM)
    return pl.pallas_call(
        lump_kernel,
        out_shape=[jax.ShapeDtypeStruct((rows, n), pieces[0].dtype) for n in SPLITS],
        in_specs=[vmem] * len(pieces),
        out_specs=[vmem] * len(SPLITS),
        cost_estimate=pl.CostEstimate(
            flops=0, bytes_accessed=4 * rows * sum(SPLITS), transcendentals=0
        ),
    )(*pieces)


def transpose_kernel(acts_ref, after_ref, out_ref):
    owner_rows = out_ref.shape[1] // NZ
    for at in range(0, acts_ref.shape[1], 128):
        turned = acts_ref[:, at : at + 128].T
        for low in range(0, 128, owner_rows):
            piece = (at + low) // owner_rows
            y, z, x = piece // (NZ * NX), piece // NX % NZ, piece % NX
            out_ref[y * NX + x, z * owner_rows : (z + 1) * owner_rows, :] = turned[
                low : low + owner_rows
            ]


def transpose(acts, after):
    tok_count, model_width = acts.shape
    vmem = pl.BlockSpec(memory_space=pltpu.VMEM)
    return pl.pallas_call(
        transpose_kernel,
        out_shape=jax.ShapeDtypeStruct(
            (NX * NY, model_width // (NX * NY), tok_count), acts.dtype
        ),
        in_specs=[vmem, pl.BlockSpec(memory_space=pl.ANY)],
        out_specs=vmem,
        compiler_params=pltpu.CompilerParams(vmem_limit_bytes=24 * 1024 * 1024),
        cost_estimate=pl.CostEstimate(
            flops=acts.size, bytes_accessed=4 * acts.size, transcendentals=0
        ),
    )(acts, after)


def dot_kernel(offsets, has_start, index_ref, acts_ref, other_ref, *refs):
    out_ref = refs[-1]
    start_ref = refs[0] if has_start else None
    parts = refs[1:-1] if has_start else refs[:-1]
    tile = 128
    for row in range(0, out_ref.shape[0], tile):
        cut = pl.ds(row, tile)
        total = start_ref[cut, :] if has_start else None
        for part_ref, places in zip(parts, offsets):
            blocks = []
            for place in places:
                block = index_ref[place]
                blocks += [acts_ref[block, cut, :], other_ref[block, cut, :]]
            product = jnp.dot(
                jnp.concatenate(blocks, axis=1), part_ref[...], preferred_element_type=jnp.float32
            )
            total = product if total is None else total + product
        out_ref[cut, :] = total


def multiply(index, acts, other, parts, offsets, start=None):
    width, n = acts.shape[1], parts[0].shape[1]
    operands = [acts, other] + ([] if start is None else [start]) + list(parts)
    depth = sum(part.shape[0] for part in parts)
    vmem = pl.BlockSpec(memory_space=pltpu.VMEM)

    def kernel(*refs):
        read = refs[: 1 + len(operands)]
        dot_kernel(offsets, start is not None, *read, refs[-1])

    return pl.pallas_call(
        kernel,
        out_shape=jax.ShapeDtypeStruct((width, n), jnp.float32),
        in_specs=[pl.BlockSpec(memory_space=pltpu.SMEM)]
        + [vmem] * len(operands),
        out_specs=vmem,
        compiler_params=pltpu.CompilerParams(vmem_limit_bytes=40 * 1024 * 1024),
        cost_estimate=pl.CostEstimate(
            flops=2 * width * n * depth, bytes_accessed=2 * depth * (n + width), transcendentals=0
        ),
    )(index, *operands)


def sum_all(value):
    rows = jnp.broadcast_to(value, (DEVICES, 1, 128))
    return jnp.sum(lax.all_to_all(rows, AXES, split_axis=0, concat_axis=0, tiled=True)[:, 0, 0])


def body(activations, key_grads, value_grads, block_lengths):
    tok_count, model_width = activations.shape
    head_width = key_grads.shape[1]
    x, c, y, z = (lax.axis_index(axis) for axis in AXES)
    is_keys = c == 0
    position = (((x * NC + c) * NY + y) * NZ + z) * tok_count
    clip_norm = math.sqrt(2.0 * model_width * head_width)

    place = jnp.stack((c, lax.div(position, CH), lax.rem(position, CH))).astype(jnp.int32)
    mine, theirs = mask(place, block_lengths, key_grads, value_grads)
    received = swap_cores(theirs)
    mine_before, mine_after = first_ring(mine, 1), first_ring(mine, -1)
    received_before, received_after = first_ring(received, 1), first_ring(received, -1)
    mine_opposite = first_ring(mine_before, 1)
    received_opposite = first_ring(received_after, -1)
    parts = lumps(
        (
            mine,
            received,
            mine_before,
            received_before,
            mine_after,
            received_after,
            mine_opposite,
            received_opposite,
        )
    )

    across = transpose(activations, mine_before)
    acts = lax.all_to_all(across, ("y", "x"), split_axis=0, concat_axis=0, tiled=True)
    other = swap_cores(acts)

    first, second = jnp.where(is_keys, x, y), jnp.where(is_keys, y, x)
    index = []
    for offset2 in OFFSETS:
        for offset1 in OFFSETS:
            at1, at2 = lax.rem(first + offset1 + 4, 4), lax.rem(second + offset2 + 4, 4)
            index.append(jnp.where(is_keys, at2 * NX + at1, at1 * NX + at2))
    index = jnp.stack(index).astype(jnp.int32)
    own, minus, plus, across_ring = (tuple(range(4 * i, 4 * i + 4)) for i in range(4))

    owned = []
    for part, lump in enumerate(parts):
        step = 1 if part % 2 == 0 else -1
        lump_before = second_ring(lump, 1)
        lump_after = second_ring(lump, -1)
        lump_opposite = second_ring(lump_before if step == 1 else lump_after, step)
        weight = multiply(
            index, acts, other, [lump, lump_before, lump_after], [own, minus, plus]
        )
        weight = multiply(index, acts, other, [lump_opposite], [across_ring], weight)
        owned.append(lax.psum_scatter(weight, "z", scatter_dimension=0, tiled=True))

    total = sum_all(sum(jnp.sum(part * part) for part in owned))
    owned = jnp.concatenate(owned, axis=1)
    half = owned.shape[0] // 2
    upper, lower = owned[:half], owned[half:]
    kept = jnp.where(is_keys, upper, lower)
    swapped = swap_cores(jnp.where(is_keys, lower, upper))
    factor = jnp.minimum(1.0, clip_norm / jnp.sqrt(total))
    key_clipped = (jnp.where(is_keys, kept, swapped) * factor).astype(jnp.bfloat16)
    value_clipped = (jnp.where(is_keys, swapped, kept) * factor).astype(jnp.bfloat16)
    return key_clipped, value_clipped


def solution(mesh):
    fine = Mesh(mesh.devices.reshape(NX, NC, NY, NZ), AXES)
    tokens = P(AXES, None)
    owners = P(("y", "z", "x", "c"), None)
    return jax.shard_map(
        body,
        mesh=fine,
        in_specs=(tokens, tokens, tokens, P()),
        out_specs=(owners, owners),
        check_vma=False,
    )
```

```python
import functools
import itertools
import math

import jax
import jax.numpy as jnp
from jax import lax
from jax.experimental import pallas as pl
from jax.experimental.pallas import tpu as pltpu
from jax.sharding import Mesh, PartitionSpec as P

CH = 512
AXES = ("x", "c", "y", "z")
NX, NC, NY, NZ = 4, 2, 4, 8
DEVICES = NX * NC * NY * NZ
OFFSETS = (0, -1, 1, 2)
COLUMNS = 256


def pairs(move):
    out = []
    for x, c, y, z in itertools.product(range(NX), range(NC), range(NY), range(NZ)):
        tx, tc, ty, tz = move(x, c, y, z)
        source = ((x * NC + c) * NY + y) * NZ + z
        target = (((tx % NX) * NC + tc % NC) * NY + ty % NY) * NZ + tz % NZ
        out.append((source, target))
    return out


def send(value, move):
    return lax.ppermute(value, AXES, pairs(move))


def swap_cores(value):
    return send(value, lambda x, c, y, z: (x, 1 - c, y, z))


def first_ring(value, step):
    return send(value, lambda x, c, y, z: (x + step, c, y, z) if c == 0 else (x, c, y + step, z))


def second_ring(value, step):
    return send(value, lambda x, c, y, z: (x, c, y + step, z) if c == 0 else (x + step, c, y, z))


def z_ring(value, step):
    return send(value, lambda x, c, y, z: (x, c, y, z + step))


VMEM = pl.BlockSpec(memory_space=pltpu.VMEM)
SMEM = pl.BlockSpec(memory_space=pltpu.SMEM)
ANY = pl.BlockSpec(memory_space=pl.ANY)


def mask_kernel(place_ref, lengths_ref, keys_ref, values_ref, mine_ref, theirs_ref):
    is_keys = place_ref[0] == 0
    limit = lengths_ref[place_ref[1]] - place_ref[2]
    keys, values = keys_ref[...], values_ref[...]
    rows = lax.broadcasted_iota(jnp.int32, keys.shape, 0)
    zero = jnp.zeros_like(keys)
    keys = jnp.where(rows < limit, keys, zero)
    values = jnp.where(rows < limit, values, zero)
    mine_ref[...] = jnp.where(is_keys, keys, values)
    theirs_ref[...] = jnp.where(is_keys, values, keys)


def mask(place, block_lengths, key_grads, value_grads):
    return pl.pallas_call(
        mask_kernel,
        out_shape=[jax.ShapeDtypeStruct(key_grads.shape, key_grads.dtype)] * 2,
        in_specs=[SMEM, SMEM, VMEM, VMEM],
        out_specs=[VMEM, VMEM],
        cost_estimate=pl.CostEstimate(
            flops=key_grads.size, bytes_accessed=8 * key_grads.size, transcendentals=0
        ),
    )(place, block_lengths, key_grads, value_grads)


def stack(pieces):
    tok_count, width = pieces[0].shape
    half = len(pieces) // 2

    def kernel(*refs):
        for i, piece_ref in enumerate(refs[:-2]):
            refs[-2 + i // half][pl.ds(i % half * tok_count, tok_count), :] = piece_ref[...]

    return pl.pallas_call(
        kernel,
        out_shape=[jax.ShapeDtypeStruct((half * tok_count, width), pieces[0].dtype)] * 2,
        in_specs=[VMEM] * len(pieces),
        out_specs=[VMEM] * 2,
        cost_estimate=pl.CostEstimate(
            flops=0, bytes_accessed=8 * half * tok_count * width, transcendentals=0
        ),
    )(*pieces)


def transpose_kernel(acts_ref, out_ref):
    owner_rows = out_ref.shape[1] // NZ
    for at in range(0, acts_ref.shape[1], 128):
        turned = acts_ref[:, at : at + 128].T
        for low in range(0, 128, owner_rows):
            piece = (at + low) // owner_rows
            y, z, x = piece // (NZ * NX), piece // NX % NZ, piece % NX
            out_ref[y * NX + x, z * owner_rows : (z + 1) * owner_rows, :] = turned[
                low : low + owner_rows
            ]


def transpose(acts):
    tok_count, model_width = acts.shape
    return pl.pallas_call(
        transpose_kernel,
        out_shape=jax.ShapeDtypeStruct(
            (NX * NY, model_width // (NX * NY), tok_count), acts.dtype
        ),
        in_specs=[VMEM],
        out_specs=VMEM,
        compiler_params=pltpu.CompilerParams(vmem_limit_bytes=24 * 1024 * 1024),
        cost_estimate=pl.CostEstimate(
            flops=acts.size, bytes_accessed=4 * acts.size, transcendentals=0
        ),
    )(acts)


def choose(index, acts, other):
    blocks, width, tok_count = acts.shape

    def kernel(index_ref, acts_ref, other_ref, out_ref):
        for at in range(blocks):
            low = at % 2 * 2 * tok_count
            block = index_ref[at]
            out_ref[at // 2, :, low : low + tok_count] = acts_ref[block]
            out_ref[at // 2, :, low + tok_count : low + 2 * tok_count] = other_ref[block]

    return pl.pallas_call(
        kernel,
        out_shape=jax.ShapeDtypeStruct((blocks // 2, width, 4 * tok_count), acts.dtype),
        in_specs=[SMEM, VMEM, VMEM],
        out_specs=VMEM,
        compiler_params=pltpu.CompilerParams(vmem_limit_bytes=24 * 1024 * 1024),
        cost_estimate=pl.CostEstimate(
            flops=0, bytes_accessed=8 * acts.size, transcendentals=0
        ),
    )(index, acts, other)


def multiply(chosen, parts, first, start=None):
    _, width, depth = chosen.shape
    n = parts[0].shape[1]
    count = len(parts)

    def kernel(chosen_ref, *refs):
        total = None if start is None else refs[count][...]
        for part in range(count):
            product = jnp.dot(
                chosen_ref[part], refs[part][...], preferred_element_type=jnp.float32
            )
            total = product if total is None else total + product
        refs[-1][...] = total

    columns = pl.BlockSpec((width, COLUMNS), lambda i: (0, i))
    return pl.pallas_call(
        kernel,
        out_shape=jax.ShapeDtypeStruct((width, n), jnp.float32),
        grid=(n // COLUMNS,),
        in_specs=[pl.BlockSpec((count, width, depth), lambda i: (first // count, 0, 0))]
        + [pl.BlockSpec((depth, COLUMNS), lambda i: (0, i))] * count
        + ([] if start is None else [columns]),
        out_specs=columns,
        compiler_params=pltpu.CompilerParams(vmem_limit_bytes=32 * 1024 * 1024),
        cost_estimate=pl.CostEstimate(
            flops=2 * width * n * depth * count,
            bytes_accessed=2 * depth * count * (n + width),
            transcendentals=0,
        ),
    )(chosen, *parts, *(() if start is None else (start,)))


def reduce_z(partial, z):
    rows = partial.shape[0] // NZ
    half = rows // 2

    def block(offset):
        return lax.dynamic_slice_in_dim(partial, lax.rem(z + offset + NZ, NZ) * rows, rows, axis=0)

    far = block(4)
    up = z_ring(far[:half], 1)
    down = z_ring(far[half:], -1)
    near_up, near_down = block(3), block(-3)
    up = z_ring(jnp.concatenate((near_up[:half] + up, near_up[half:]), axis=0), 1)
    down = z_ring(jnp.concatenate((near_down[:half], near_down[half:] + down), axis=0), -1)
    for offset in (2, 1):
        up = z_ring(block(offset) + up, 1)
        down = z_ring(block(-offset) + down, -1)
    return block(0) + up + down


def sum_all(value):
    rows = jnp.broadcast_to(value, (DEVICES, 1, 128))
    return jnp.sum(lax.all_to_all(rows, AXES, split_axis=0, concat_axis=0, tiled=True)[:, 0, 0])


def body(activations, key_grads, value_grads, block_lengths):
    tok_count, model_width = activations.shape
    head_width = key_grads.shape[1]
    x, c, y, z = (lax.axis_index(axis) for axis in AXES)
    is_keys = c == 0
    position = (((x * NC + c) * NY + y) * NZ + z) * tok_count
    clip_norm = math.sqrt(2.0 * model_width * head_width)

    place = jnp.stack((c, lax.div(position, CH), lax.rem(position, CH))).astype(jnp.int32)
    mine, theirs = mask(place, block_lengths, key_grads, value_grads)
    received = swap_cores(theirs)
    mine_before, mine_after = first_ring(mine, 1), first_ring(mine, -1)
    received_before, received_after = first_ring(received, 1), first_ring(received, -1)
    pieces = (mine, received, mine_before, received_before, mine_after, received_after)
    pieces += (first_ring(mine_before, 1), first_ring(received_after, -1))

    across, *_ = lax.optimization_barrier((transpose(activations), *pieces))
    acts = lax.all_to_all(across, ("y", "x"), split_axis=0, concat_axis=0, tiled=True)

    first, second = jnp.where(is_keys, x, y), jnp.where(is_keys, y, x)
    index = []
    for offset2 in OFFSETS:
        for offset1 in OFFSETS:
            at1, at2 = lax.rem(first + offset1 + 4, 4), lax.rem(second + offset2 + 4, 4)
            index.append(jnp.where(is_keys, at2 * NX + at1, at1 * NX + at2))
    index = jnp.stack(index).astype(jnp.int32)

    upper, lower = stack(pieces)
    upper_before, upper_after = second_ring(upper, 1), second_ring(upper, -1)
    lower_before, lower_after = second_ring(lower, 1), second_ring(lower, -1)
    acts, upper_before, upper_after, lower_before, lower_after = lax.optimization_barrier(
        (acts, upper_before, upper_after, lower_before, lower_after)
    )
    chosen = choose(index, acts, swap_cores(acts))
    opposite = [second_ring(upper_before, 1), second_ring(lower_after, -1)]
    direct = [upper, lower, upper_before, lower_before, upper_after, lower_after]
    weight = multiply(chosen, direct, 0)
    weight = multiply(chosen, opposite, 6, weight)
    owned = reduce_z(weight, z)

    total = sum_all(jnp.sum(owned * owned))
    half = owned.shape[0] // 2
    kept = jnp.where(is_keys, owned[:half], owned[half:])
    swapped = swap_cores(jnp.where(is_keys, owned[half:], owned[:half]))
    factor = jnp.minimum(1.0, clip_norm / jnp.sqrt(total))
    key_clipped = (jnp.where(is_keys, kept, swapped) * factor).astype(jnp.bfloat16)
    value_clipped = (jnp.where(is_keys, swapped, kept) * factor).astype(jnp.bfloat16)
    return key_clipped, value_clipped


def solution(mesh):
    fine = Mesh(mesh.devices.reshape(NX, NC, NY, NZ), AXES)
    tokens = P(AXES, None)
    owners = P(("y", "z", "x", "c"), None)
    return jax.shard_map(
        body,
        mesh=fine,
        in_specs=(tokens, tokens, tokens, P()),
        out_specs=(owners, owners),
        check_vma=False,
    )
```

```python
import functools
import itertools
import math

import jax
import jax.numpy as jnp
from jax import lax
from jax.experimental import pallas as pl
from jax.experimental.pallas import tpu as pltpu
from jax.sharding import Mesh, PartitionSpec as P

CH = 512
AXES = ("x", "c", "y", "z")
NX, NC, NY, NZ = 4, 2, 4, 8
DEVICES = NX * NC * NY * NZ
OFFSETS = (0, -1, 1, 2)
COLUMNS = 256


def pairs(move):
    out = []
    for x, c, y, z in itertools.product(range(NX), range(NC), range(NY), range(NZ)):
        tx, tc, ty, tz = move(x, c, y, z)
        source = ((x * NC + c) * NY + y) * NZ + z
        target = (((tx % NX) * NC + tc % NC) * NY + ty % NY) * NZ + tz % NZ
        out.append((source, target))
    return out


def send(value, move):
    return lax.ppermute(value, AXES, pairs(move))


def swap_cores(value):
    return send(value, lambda x, c, y, z: (x, 1 - c, y, z))


def first_ring(value, step):
    return send(value, lambda x, c, y, z: (x + step, c, y, z) if c == 0 else (x, c, y + step, z))


def second_ring(value, step):
    return send(value, lambda x, c, y, z: (x, c, y + step, z) if c == 0 else (x + step, c, y, z))


def z_ring(value, step):
    return send(value, lambda x, c, y, z: (x, c, y, z + step))


VMEM = pl.BlockSpec(memory_space=pltpu.VMEM)
SMEM = pl.BlockSpec(memory_space=pltpu.SMEM)
ANY = pl.BlockSpec(memory_space=pl.ANY)


def mask_kernel(place_ref, lengths_ref, keys_ref, values_ref, mine_ref, theirs_ref):
    is_keys = place_ref[0] == 0
    limit = lengths_ref[place_ref[1]] - place_ref[2]
    keys, values = keys_ref[...], values_ref[...]
    rows = lax.broadcasted_iota(jnp.int32, keys.shape, 0)
    zero = jnp.zeros_like(keys)
    keys = jnp.where(rows < limit, keys, zero)
    values = jnp.where(rows < limit, values, zero)
    mine_ref[...] = jnp.where(is_keys, keys, values)
    theirs_ref[...] = jnp.where(is_keys, values, keys)


def mask(place, block_lengths, key_grads, value_grads):
    return pl.pallas_call(
        mask_kernel,
        out_shape=[jax.ShapeDtypeStruct(key_grads.shape, key_grads.dtype)] * 2,
        in_specs=[SMEM, SMEM, VMEM, VMEM],
        out_specs=[VMEM, VMEM],
        cost_estimate=pl.CostEstimate(
            flops=key_grads.size, bytes_accessed=8 * key_grads.size, transcendentals=0
        ),
    )(place, block_lengths, key_grads, value_grads)


def stack(pieces):
    tok_count, width = pieces[0].shape
    half = len(pieces) // 2

    def kernel(*refs):
        for i, piece_ref in enumerate(refs[:-2]):
            refs[-2 + i // half][pl.ds(i % half * tok_count, tok_count), :] = piece_ref[...]

    return pl.pallas_call(
        kernel,
        out_shape=[jax.ShapeDtypeStruct((half * tok_count, width), pieces[0].dtype)] * 2,
        in_specs=[VMEM] * len(pieces),
        out_specs=[VMEM] * 2,
        cost_estimate=pl.CostEstimate(
            flops=0, bytes_accessed=8 * half * tok_count * width, transcendentals=0
        ),
    )(*pieces)


def transpose_kernel(acts_ref, out_ref):
    owner_rows = out_ref.shape[1] // NZ
    for at in range(0, acts_ref.shape[1], 128):
        turned = acts_ref[:, at : at + 128].T
        for low in range(0, 128, owner_rows):
            piece = (at + low) // owner_rows
            y, z, x = piece // (NZ * NX), piece // NX % NZ, piece % NX
            out_ref[y * NX + x, z * owner_rows : (z + 1) * owner_rows, :] = turned[
                low : low + owner_rows
            ]


def transpose(acts):
    tok_count, model_width = acts.shape
    return pl.pallas_call(
        transpose_kernel,
        out_shape=jax.ShapeDtypeStruct(
            (NX * NY, model_width // (NX * NY), tok_count), acts.dtype
        ),
        in_specs=[VMEM],
        out_specs=VMEM,
        compiler_params=pltpu.CompilerParams(vmem_limit_bytes=24 * 1024 * 1024),
        cost_estimate=pl.CostEstimate(
            flops=acts.size, bytes_accessed=4 * acts.size, transcendentals=0
        ),
    )(acts)


def choose(index, acts, other):
    blocks, width, tok_count = acts.shape

    def kernel(index_ref, acts_ref, other_ref, out_ref):
        for at in range(blocks):
            low = at % 2 * 2 * tok_count
            block = index_ref[at]
            out_ref[at // 2, :, low : low + tok_count] = acts_ref[block]
            out_ref[at // 2, :, low + tok_count : low + 2 * tok_count] = other_ref[block]

    return pl.pallas_call(
        kernel,
        out_shape=jax.ShapeDtypeStruct((blocks // 2, width, 4 * tok_count), acts.dtype),
        in_specs=[SMEM, VMEM, VMEM],
        out_specs=VMEM,
        compiler_params=pltpu.CompilerParams(vmem_limit_bytes=24 * 1024 * 1024),
        cost_estimate=pl.CostEstimate(
            flops=0, bytes_accessed=8 * acts.size, transcendentals=0
        ),
    )(index, acts, other)


def multiply(chosen, parts, first, start=None):
    _, width, depth = chosen.shape
    n = parts[0].shape[1]
    count = len(parts)

    def kernel(chosen_ref, *refs):
        total = None if start is None else refs[count][...]
        for part in range(count):
            product = jnp.dot(
                chosen_ref[part], refs[part][...], preferred_element_type=jnp.float32
            )
            total = product if total is None else total + product
        refs[-1][...] = total

    columns = pl.BlockSpec((width, COLUMNS), lambda i: (0, i))
    return pl.pallas_call(
        kernel,
        out_shape=jax.ShapeDtypeStruct((width, n), jnp.float32),
        grid=(n // COLUMNS,),
        in_specs=[pl.BlockSpec((count, width, depth), lambda i: (first // count, 0, 0))]
        + [pl.BlockSpec((depth, COLUMNS), lambda i: (0, i))] * count
        + ([] if start is None else [columns]),
        out_specs=columns,
        compiler_params=pltpu.CompilerParams(vmem_limit_bytes=32 * 1024 * 1024),
        cost_estimate=pl.CostEstimate(
            flops=2 * width * n * depth * count,
            bytes_accessed=2 * depth * count * (n + width),
            transcendentals=0,
        ),
    )(chosen, *parts, *(() if start is None else (start,)))


def z_block(partial, z, offset):
    rows = partial.shape[0] // NZ
    return lax.dynamic_slice_in_dim(partial, lax.rem(z + offset + NZ, NZ) * rows, rows, axis=0)


def z_step(partial, z, offset, moving=None):
    up, down = z_block(partial, z, offset), z_block(partial, z, -offset)
    half = up.shape[0] // 2
    if offset == 4:
        up, down = up[:half], down[half:]
    elif offset == 3:
        up = jnp.concatenate((up[:half] + moving[0], up[half:]), axis=0)
        down = jnp.concatenate((down[:half], down[half:] + moving[1]), axis=0)
    else:
        up, down = up + moving[0], down + moving[1]
    return z_ring(up, 1), z_ring(down, -1)


def sum_all(squares):
    rows = jnp.broadcast_to(squares[None], (DEVICES, 1, 128))
    return jnp.sum(lax.all_to_all(rows, AXES, split_axis=0, concat_axis=0, tiled=True))


def body(activations, key_grads, value_grads, block_lengths):
    tok_count, model_width = activations.shape
    head_width = key_grads.shape[1]
    x, c, y, z = (lax.axis_index(axis) for axis in AXES)
    is_keys = c == 0
    position = (((x * NC + c) * NY + y) * NZ + z) * tok_count
    clip_norm = math.sqrt(2.0 * model_width * head_width)

    place = jnp.stack((c, lax.div(position, CH), lax.rem(position, CH))).astype(jnp.int32)
    mine, theirs = mask(place, block_lengths, key_grads, value_grads)
    received = swap_cores(theirs)
    mine_before, mine_after = first_ring(mine, 1), first_ring(mine, -1)
    received_before, received_after = first_ring(received, 1), first_ring(received, -1)
    pieces = (mine, received, mine_before, received_before, mine_after, received_after)
    pieces += (first_ring(mine_before, 1), first_ring(received_after, -1))

    across, *_ = lax.optimization_barrier((transpose(activations), *pieces))
    acts = lax.all_to_all(across, ("y", "x"), split_axis=0, concat_axis=0, tiled=True)

    first, second = jnp.where(is_keys, x, y), jnp.where(is_keys, y, x)
    index = []
    for offset2 in OFFSETS:
        for offset1 in OFFSETS:
            at1, at2 = lax.rem(first + offset1 + 4, 4), lax.rem(second + offset2 + 4, 4)
            index.append(jnp.where(is_keys, at2 * NX + at1, at1 * NX + at2))
    index = jnp.stack(index).astype(jnp.int32)

    upper, lower = stack(pieces)
    upper_before, upper_after = second_ring(upper, 1), second_ring(upper, -1)
    lower_before, lower_after = second_ring(lower, 1), second_ring(lower, -1)
    acts, upper_before, upper_after, lower_before, lower_after = lax.optimization_barrier(
        (acts, upper_before, upper_after, lower_before, lower_after)
    )
    chosen = choose(index, acts, swap_cores(acts))
    opposite = [second_ring(upper_before, 1), second_ring(lower_after, -1)]
    direct = [upper, lower, upper_before, lower_before, upper_after, lower_after]
    weight = multiply(chosen, direct, 0)
    weight = multiply(chosen, opposite, 6, weight)
    streams = jnp.split(weight, 2, axis=1)
    moving = [None] * len(streams)
    for offset in (4, 3, 2, 1):
        moving = [z_step(part, z, offset, old) for part, old in zip(streams, moving)]
    owned = jnp.concatenate(
        [z_block(part, z, 0) + up + down for part, (up, down) in zip(streams, moving)], axis=1
    )

    squares = jnp.sum((owned * owned).reshape(-1, 128), axis=0)
    total = sum_all(squares[None])
    half = owned.shape[0] // 2
    kept = jnp.where(is_keys, owned[:half], owned[half:])
    swapped = swap_cores(jnp.where(is_keys, owned[half:], owned[:half]))
    factor = jnp.minimum(1.0, clip_norm / jnp.sqrt(total))
    key_clipped = (jnp.where(is_keys, kept, swapped) * factor).astype(jnp.bfloat16)
    value_clipped = (jnp.where(is_keys, swapped, kept) * factor).astype(jnp.bfloat16)
    return key_clipped, value_clipped


def solution(mesh):
    fine = Mesh(mesh.devices.reshape(NX, NC, NY, NZ), AXES)
    tokens = P(AXES, None)
    owners = P(("y", "z", "x", "c"), None)
    return jax.shard_map(
        body,
        mesh=fine,
        in_specs=(tokens, tokens, tokens, P()),
        out_specs=(owners, owners),
        check_vma=False,
    )
```

```python
import functools
import itertools
import math

import jax
import jax.numpy as jnp
from jax import lax
from jax.experimental import pallas as pl
from jax.experimental.pallas import tpu as pltpu
from jax.sharding import Mesh, PartitionSpec as P

CH = 512
AXES = ("x", "c", "y", "z")
NX, NC, NY, NZ = 4, 2, 4, 8
DEVICES = NX * NC * NY * NZ
OFFSETS = (0, -1, 1, 2)
COLUMNS = 256


def pairs(move):
    out = []
    for x, c, y, z in itertools.product(range(NX), range(NC), range(NY), range(NZ)):
        tx, tc, ty, tz = move(x, c, y, z)
        source = ((x * NC + c) * NY + y) * NZ + z
        target = (((tx % NX) * NC + tc % NC) * NY + ty % NY) * NZ + tz % NZ
        out.append((source, target))
    return out


def send(value, move):
    return lax.ppermute(value, AXES, pairs(move))


def swap_cores(value):
    return send(value, lambda x, c, y, z: (x, 1 - c, y, z))


def first_ring(value, step):
    return send(value, lambda x, c, y, z: (x + step, c, y, z) if c == 0 else (x, c, y + step, z))


def second_ring(value, step):
    return send(value, lambda x, c, y, z: (x, c, y + step, z) if c == 0 else (x + step, c, y, z))


def z_ring(value, step):
    return send(value, lambda x, c, y, z: (x, c, y, z + step))


VMEM = pl.BlockSpec(memory_space=pltpu.VMEM)
SMEM = pl.BlockSpec(memory_space=pltpu.SMEM)
ANY = pl.BlockSpec(memory_space=pl.ANY)


def mask_kernel(lengths_ref, keys_ref, values_ref, mine_ref, theirs_ref):
    x, c, y, z = (lax.axis_index(axis) for axis in AXES)
    is_keys = c == 0
    position = (((x * NC + c) * NY + y) * NZ + z) * keys_ref.shape[0]
    limit = lengths_ref[position // CH] - position % CH
    keys, values = keys_ref[...], values_ref[...]
    rows = lax.broadcasted_iota(jnp.int32, keys.shape, 0)
    zero = jnp.zeros_like(keys)
    keys = jnp.where(rows < limit, keys, zero)
    values = jnp.where(rows < limit, values, zero)
    mine_ref[...] = jnp.where(is_keys, keys, values)
    theirs_ref[...] = jnp.where(is_keys, values, keys)


def mask(block_lengths, key_grads, value_grads):
    return pl.pallas_call(
        mask_kernel,
        out_shape=[jax.ShapeDtypeStruct(key_grads.shape, key_grads.dtype)] * 2,
        in_specs=[SMEM, VMEM, VMEM],
        out_specs=[VMEM, VMEM],
        cost_estimate=pl.CostEstimate(
            flops=key_grads.size, bytes_accessed=8 * key_grads.size, transcendentals=0
        ),
    )(block_lengths, key_grads, value_grads)


def stack(pieces):
    tok_count, width = pieces[0].shape
    half, n = len(pieces) // 2, width // 2

    def kernel(*refs):
        for i, piece_ref in enumerate(refs[:-4]):
            place = pl.ds(i % half * tok_count, tok_count)
            refs[-4 + i // half][place, :] = piece_ref[:, pl.ds(0, n)]
            refs[-2 + i // half][place, :] = piece_ref[:, pl.ds(n, n)]

    return pl.pallas_call(
        kernel,
        out_shape=[jax.ShapeDtypeStruct((half * tok_count, n), pieces[0].dtype)] * 4,
        in_specs=[VMEM] * len(pieces),
        out_specs=[VMEM] * 4,
        cost_estimate=pl.CostEstimate(
            flops=0, bytes_accessed=8 * half * tok_count * width, transcendentals=0
        ),
    )(*pieces)


def transpose_kernel(acts_ref, out_ref):
    owner_rows = out_ref.shape[1] // NZ
    for at in range(0, acts_ref.shape[1], 128):
        turned = acts_ref[:, at : at + 128].T
        for low in range(0, 128, owner_rows):
            piece = (at + low) // owner_rows
            y, z, x = piece // (NZ * NX), piece // NX % NZ, piece % NX
            out_ref[y * NX + x, z * owner_rows : (z + 1) * owner_rows, :] = turned[
                low : low + owner_rows
            ]


def transpose(acts):
    tok_count, model_width = acts.shape
    return pl.pallas_call(
        transpose_kernel,
        out_shape=jax.ShapeDtypeStruct(
            (NX * NY, model_width // (NX * NY), tok_count), acts.dtype
        ),
        in_specs=[VMEM],
        out_specs=VMEM,
        compiler_params=pltpu.CompilerParams(vmem_limit_bytes=24 * 1024 * 1024),
        cost_estimate=pl.CostEstimate(
            flops=acts.size, bytes_accessed=4 * acts.size, transcendentals=0
        ),
    )(acts)


def choose(index, acts, other):
    blocks, width, tok_count = acts.shape

    def kernel(index_ref, acts_ref, other_ref, out_ref):
        for at in range(blocks):
            low = at % 2 * 2 * tok_count
            block = index_ref[at]
            out_ref[at // 2, :, low : low + tok_count] = acts_ref[block]
            out_ref[at // 2, :, low + tok_count : low + 2 * tok_count] = other_ref[block]

    return pl.pallas_call(
        kernel,
        out_shape=jax.ShapeDtypeStruct((blocks // 2, width, 4 * tok_count), acts.dtype),
        in_specs=[SMEM, VMEM, VMEM],
        out_specs=VMEM,
        compiler_params=pltpu.CompilerParams(vmem_limit_bytes=24 * 1024 * 1024),
        cost_estimate=pl.CostEstimate(
            flops=0, bytes_accessed=8 * acts.size, transcendentals=0
        ),
    )(index, acts, other)


def multiply(chosen, parts, first, start=None):
    _, width, depth = chosen.shape
    n = parts[0].shape[1]
    count = len(parts)

    def kernel(chosen_ref, *refs):
        total = None if start is None else refs[count][...]
        for part in range(count):
            product = jnp.dot(
                chosen_ref[part], refs[part][...], preferred_element_type=jnp.float32
            )
            total = product if total is None else total + product
        refs[-1][...] = total

    return pl.pallas_call(
        kernel,
        out_shape=jax.ShapeDtypeStruct((width, n), jnp.float32),
        grid=(n // COLUMNS,),
        in_specs=[pl.BlockSpec((count, width, depth), lambda i: (first // count, 0, 0))]
        + [pl.BlockSpec((depth, COLUMNS), lambda i: (0, i))] * count
        + ([] if start is None else [pl.BlockSpec((width, COLUMNS), lambda i: (0, i))]),
        out_specs=pl.BlockSpec((width, COLUMNS), lambda i: (0, i)),
        compiler_params=pltpu.CompilerParams(vmem_limit_bytes=32 * 1024 * 1024),
        cost_estimate=pl.CostEstimate(
            flops=2 * width * n * depth * count,
            bytes_accessed=2 * depth * count * (n + width),
            transcendentals=0,
        ),
    )(chosen, *parts, *(() if start is None else (start,)))


def z_block(partial, z, offset):
    rows = partial.shape[0] // NZ
    return lax.dynamic_slice_in_dim(partial, lax.rem(z + offset + NZ, NZ) * rows, rows, axis=0)


def z_step(partial, z, offset, moving=None):
    up, down = z_block(partial, z, offset), z_block(partial, z, -offset)
    half = up.shape[0] // 2
    if offset == 4:
        up, down = up[:half], down[half:]
    elif offset == 3:
        up = jnp.concatenate((up[:half] + moving[0], up[half:]), axis=0)
        down = jnp.concatenate((down[:half], down[half:] + moving[1]), axis=0)
    else:
        up, down = up + moving[0], down + moving[1]
    return lax.optimization_barrier((z_ring(up, 1), z_ring(down, -1)))


def sum_all(squares):
    rows = jnp.broadcast_to(squares[None], (DEVICES, 1, 128))
    return jnp.sum(lax.all_to_all(rows, AXES, split_axis=0, concat_axis=0, tiled=True))


def body(activations, key_grads, value_grads, block_lengths):
    tok_count, model_width = activations.shape
    head_width = key_grads.shape[1]
    x, c, y, z = (lax.axis_index(axis) for axis in AXES)
    is_keys = c == 0
    clip_norm = math.sqrt(2.0 * model_width * head_width)

    mine, theirs = mask(block_lengths, key_grads, value_grads)
    received = swap_cores(theirs)
    mine_before, mine_after = first_ring(mine, 1), first_ring(mine, -1)
    received_before, received_after = first_ring(received, 1), first_ring(received, -1)
    pieces = (mine, received, mine_before, received_before, mine_after, received_after)
    pieces += (first_ring(mine_before, 1), first_ring(received_after, -1))

    across, *_ = lax.optimization_barrier((transpose(activations), *pieces))
    acts = lax.all_to_all(across, ("y", "x"), split_axis=0, concat_axis=0, tiled=True)

    first, second = jnp.where(is_keys, x, y), jnp.where(is_keys, y, x)
    index = []
    for offset2 in OFFSETS:
        for offset1 in OFFSETS:
            at1, at2 = lax.rem(first + offset1 + 4, 4), lax.rem(second + offset2 + 4, 4)
            index.append(jnp.where(is_keys, at2 * NX + at1, at1 * NX + at2))
    index = jnp.stack(index).astype(jnp.int32)

    stacked = stack(pieces)
    direct = [second_ring(part, step) for part in stacked for step in (1, -1)]
    acts, *direct = lax.optimization_barrier((acts, *direct))
    chosen = choose(index, acts, swap_cores(acts))
    streams = []
    for (upper, lower), sent in ((stacked[:2], direct[:4]), (stacked[2:], direct[4:])):
        opposite = [second_ring(sent[0], 1), second_ring(sent[3], -1)]
        near = [upper, lower, sent[0], sent[2], sent[1], sent[3]]
        streams.append(multiply(chosen, opposite, 6, multiply(chosen, near, 0)))

    moving = [None] * len(streams)
    for offset in (4, 3, 2, 1):
        moving = [z_step(part, z, offset, old) for part, old in zip(streams, moving)]
    owned = jnp.concatenate(
        [z_block(part, z, 0) + up + down for part, (up, down) in zip(streams, moving)], axis=1
    )

    squares = jnp.sum((owned * owned).reshape(-1, 128), axis=0)
    total = sum_all(squares[None])
    half = owned.shape[0] // 2
    kept = jnp.where(is_keys, owned[:half], owned[half:])
    swapped = swap_cores(jnp.where(is_keys, owned[half:], owned[:half]))
    factor = jnp.minimum(1.0, clip_norm / jnp.sqrt(total))
    key_clipped = (jnp.where(is_keys, kept, swapped) * factor).astype(jnp.bfloat16)
    value_clipped = (jnp.where(is_keys, swapped, kept) * factor).astype(jnp.bfloat16)
    return key_clipped, value_clipped


def solution(mesh):
    fine = Mesh(mesh.devices.reshape(NX, NC, NY, NZ), AXES)
    tokens = P(AXES, None)
    owners = P(("y", "z", "x", "c"), None)
    return jax.shard_map(
        body,
        mesh=fine,
        in_specs=(tokens, tokens, tokens, P()),
        out_specs=(owners, owners),
        check_vma=False,
    )
```

```python
import functools
import itertools
import math

import jax
import jax.numpy as jnp
from jax import lax
from jax.experimental import pallas as pl
from jax.experimental.pallas import tpu as pltpu
from jax.sharding import Mesh, PartitionSpec as P

CH = 512
AXES = ("x", "c", "y", "z")
NX, NC, NY, NZ = 4, 2, 4, 8
DEVICES = NX * NC * NY * NZ
OFFSETS = (0, -1, 1, 2)
COLUMNS = 256


def pairs(move):
    out = []
    for x, c, y, z in itertools.product(range(NX), range(NC), range(NY), range(NZ)):
        tx, tc, ty, tz = move(x, c, y, z)
        source = ((x * NC + c) * NY + y) * NZ + z
        target = (((tx % NX) * NC + tc % NC) * NY + ty % NY) * NZ + tz % NZ
        out.append((source, target))
    return out


def send(value, move):
    return lax.ppermute(value, AXES, pairs(move))


def swap_cores(value):
    return send(value, lambda x, c, y, z: (x, 1 - c, y, z))


def first_ring(value, step):
    return send(value, lambda x, c, y, z: (x + step, c, y, z) if c == 0 else (x, c, y + step, z))


def second_ring(value, step):
    return send(value, lambda x, c, y, z: (x, c, y + step, z) if c == 0 else (x + step, c, y, z))


def z_ring(value, step):
    return send(value, lambda x, c, y, z: (x, c, y, z + step))


VMEM = pl.BlockSpec(memory_space=pltpu.VMEM)
SMEM = pl.BlockSpec(memory_space=pltpu.SMEM)
ANY = pl.BlockSpec(memory_space=pl.ANY)


def mask_kernel(lengths_ref, keys_ref, values_ref, mine_ref, theirs_ref):
    x, c, y, z = (lax.axis_index(axis) for axis in AXES)
    is_keys = c == 0
    position = (((x * NC + c) * NY + y) * NZ + z) * keys_ref.shape[0]
    limit = lengths_ref[position // CH] - position % CH
    keys, values = keys_ref[...], values_ref[...]
    rows = lax.broadcasted_iota(jnp.int32, keys.shape, 0)
    zero = jnp.zeros_like(keys)
    keys = jnp.where(rows < limit, keys, zero)
    values = jnp.where(rows < limit, values, zero)
    mine_ref[...] = jnp.where(is_keys, keys, values)
    theirs_ref[...] = jnp.where(is_keys, values, keys)


def mask(block_lengths, key_grads, value_grads):
    return pl.pallas_call(
        mask_kernel,
        out_shape=[jax.ShapeDtypeStruct(key_grads.shape, key_grads.dtype)] * 2,
        in_specs=[SMEM, VMEM, VMEM],
        out_specs=[VMEM, VMEM],
        cost_estimate=pl.CostEstimate(
            flops=key_grads.size, bytes_accessed=8 * key_grads.size, transcendentals=0
        ),
    )(block_lengths, key_grads, value_grads)


def stack(pieces):
    tok_count, width = pieces[0].shape
    half, n = len(pieces) // 2, width // 2

    def kernel(*refs):
        for i, piece_ref in enumerate(refs[:-4]):
            place = pl.ds(i % half * tok_count, tok_count)
            refs[-4 + i // half][place, :] = piece_ref[:, pl.ds(0, n)]
            refs[-2 + i // half][place, :] = piece_ref[:, pl.ds(n, n)]

    return pl.pallas_call(
        kernel,
        out_shape=[jax.ShapeDtypeStruct((half * tok_count, n), pieces[0].dtype)] * 4,
        in_specs=[VMEM] * len(pieces),
        out_specs=[VMEM] * 4,
        cost_estimate=pl.CostEstimate(
            flops=0, bytes_accessed=8 * half * tok_count * width, transcendentals=0
        ),
    )(*pieces)


def transpose_kernel(acts_ref, out_ref):
    owner_rows = out_ref.shape[1] // NZ
    for at in range(0, acts_ref.shape[1], 128):
        turned = acts_ref[:, at : at + 128].T
        for low in range(0, 128, owner_rows):
            piece = (at + low) // owner_rows
            y, z, x = piece // (NZ * NX), piece // NX % NZ, piece % NX
            out_ref[y * NX + x, z * owner_rows : (z + 1) * owner_rows, :] = turned[
                low : low + owner_rows
            ]


def transpose(acts):
    tok_count, model_width = acts.shape
    return pl.pallas_call(
        transpose_kernel,
        out_shape=jax.ShapeDtypeStruct(
            (NX * NY, model_width // (NX * NY), tok_count), acts.dtype
        ),
        in_specs=[VMEM],
        out_specs=VMEM,
        compiler_params=pltpu.CompilerParams(vmem_limit_bytes=24 * 1024 * 1024),
        cost_estimate=pl.CostEstimate(
            flops=acts.size, bytes_accessed=4 * acts.size, transcendentals=0
        ),
    )(acts)


def choose(index, acts, other):
    blocks, width, tok_count = acts.shape

    def kernel(index_ref, acts_ref, other_ref, out_ref):
        for at in range(blocks):
            low = at % 2 * 2 * tok_count
            block = index_ref[at]
            out_ref[at // 2, :, low : low + tok_count] = acts_ref[block]
            out_ref[at // 2, :, low + tok_count : low + 2 * tok_count] = other_ref[block]

    return pl.pallas_call(
        kernel,
        out_shape=jax.ShapeDtypeStruct((blocks // 2, width, 4 * tok_count), acts.dtype),
        in_specs=[SMEM, VMEM, VMEM],
        out_specs=VMEM,
        compiler_params=pltpu.CompilerParams(vmem_limit_bytes=24 * 1024 * 1024),
        cost_estimate=pl.CostEstimate(
            flops=0, bytes_accessed=8 * acts.size, transcendentals=0
        ),
    )(index, acts, other)


def multiply(chosen, parts, first, start=None):
    _, width, depth = chosen.shape
    n = parts[0].shape[1]
    count = len(parts)

    def kernel(chosen_ref, *refs):
        total = None if start is None else refs[count][...]
        for part in range(count):
            product = jnp.dot(
                chosen_ref[part], refs[part][...], preferred_element_type=jnp.float32
            )
            total = product if total is None else total + product
        refs[-1][...] = total

    return pl.pallas_call(
        kernel,
        out_shape=jax.ShapeDtypeStruct((width, n), jnp.float32),
        grid=(n // COLUMNS,),
        in_specs=[pl.BlockSpec((count, width, depth), lambda i: (first // count, 0, 0))]
        + [pl.BlockSpec((depth, COLUMNS), lambda i: (0, i))] * count
        + ([] if start is None else [pl.BlockSpec((width, COLUMNS), lambda i: (0, i))]),
        out_specs=pl.BlockSpec((width, COLUMNS), lambda i: (0, i)),
        compiler_params=pltpu.CompilerParams(vmem_limit_bytes=32 * 1024 * 1024),
        cost_estimate=pl.CostEstimate(
            flops=2 * width * n * depth * count,
            bytes_accessed=2 * depth * count * (n + width),
            transcendentals=0,
        ),
    )(chosen, *parts, *(() if start is None else (start,)))


def z_block(partial, z, offset):
    rows = partial.shape[0] // NZ
    return lax.dynamic_slice_in_dim(partial, lax.rem(z + offset + NZ, NZ) * rows, rows, axis=0)


def z_step(partial, z, offset, moving=None):
    up, down = z_block(partial, z, offset), z_block(partial, z, -offset)
    half = up.shape[0] // 2
    if offset == 4:
        up, down = up[:half], down[half:]
    elif offset == 3:
        up = jnp.concatenate((up[:half] + moving[0], up[half:]), axis=0)
        down = jnp.concatenate((down[:half], down[half:] + moving[1]), axis=0)
    else:
        up, down = up + moving[0], down + moving[1]
    return lax.optimization_barrier((z_ring(up, 1), z_ring(down, -1)))


def sum_all(squares):
    rows = jnp.broadcast_to(squares[None], (DEVICES, 1, 128))
    return jnp.sum(lax.all_to_all(rows, AXES, split_axis=0, concat_axis=0, tiled=True))


def body(activations, key_grads, value_grads, block_lengths):
    tok_count, model_width = activations.shape
    head_width = key_grads.shape[1]
    x, c, y, z = (lax.axis_index(axis) for axis in AXES)
    is_keys = c == 0
    clip_norm = math.sqrt(2.0 * model_width * head_width)

    mine, theirs = mask(block_lengths, key_grads, value_grads)
    received = swap_cores(theirs)
    mine_before, mine_after = first_ring(mine, 1), first_ring(mine, -1)
    received_before, received_after = first_ring(received, 1), first_ring(received, -1)
    pieces = (mine, received, mine_before, received_before, mine_after, received_after)
    pieces += (first_ring(mine_before, 1), first_ring(received_after, -1))

    across, *_ = lax.optimization_barrier((transpose(activations), *pieces))
    acts = lax.all_to_all(across, ("y", "x"), split_axis=0, concat_axis=0, tiled=True)

    first, second = jnp.where(is_keys, x, y), jnp.where(is_keys, y, x)
    index = []
    for offset2 in OFFSETS:
        for offset1 in OFFSETS:
            at1, at2 = lax.rem(first + offset1 + 4, 4), lax.rem(second + offset2 + 4, 4)
            index.append(jnp.where(is_keys, at2 * NX + at1, at1 * NX + at2))
    index = jnp.stack(index).astype(jnp.int32)

    stacked = stack(pieces)
    direct = [second_ring(part, step) for part in stacked for step in (1, -1)]
    acts, *first = lax.optimization_barrier((acts, *direct[:4]))
    acts, *second = lax.optimization_barrier((acts, *direct[4:]))
    direct = first + second
    chosen = choose(index, acts, swap_cores(acts))
    streams = []
    for (upper, lower), sent in ((stacked[:2], direct[:4]), (stacked[2:], direct[4:])):
        opposite = [second_ring(sent[0], 1), second_ring(sent[3], -1)]
        near = [upper, lower, sent[0], sent[2], sent[1], sent[3]]
        streams.append(multiply(chosen, opposite, 6, multiply(chosen, near, 0)))

    moving = [None] * len(streams)
    for offset in (4, 3, 2, 1):
        moving = [z_step(part, z, offset, old) for part, old in zip(streams, moving)]
    owned = jnp.concatenate(
        [z_block(part, z, 0) + up + down for part, (up, down) in zip(streams, moving)], axis=1
    )

    squares = jnp.sum((owned * owned).reshape(-1, 128), axis=0)
    total = sum_all(squares[None])
    half = owned.shape[0] // 2
    kept = jnp.where(is_keys, owned[:half], owned[half:])
    swapped = swap_cores(jnp.where(is_keys, owned[half:], owned[:half]))
    factor = jnp.minimum(1.0, clip_norm / jnp.sqrt(total))
    key_clipped = (jnp.where(is_keys, kept, swapped) * factor).astype(jnp.bfloat16)
    value_clipped = (jnp.where(is_keys, swapped, kept) * factor).astype(jnp.bfloat16)
    return key_clipped, value_clipped


def solution(mesh):
    fine = Mesh(mesh.devices.reshape(NX, NC, NY, NZ), AXES)
    tokens = P(AXES, None)
    owners = P(("y", "z", "x", "c"), None)
    return jax.shard_map(
        body,
        mesh=fine,
        in_specs=(tokens, tokens, tokens, P()),
        out_specs=(owners, owners),
        check_vma=False,
    )
```
